32 devices in a mesh: expert: 8 (over z, y), ffn: 4 (over x, core).
Axes of the slice: x: 2, y: 2, z: 4, core: 2. Of those that a mesh axis runs over, the one named last changes fastest.
Arguments:
- tokens: bfloat16 [4096, 768], P('expert', 'ffn'), may hold values from -6 to 6
- cotangent: bfloat16 [4096, 768], P('expert', 'ffn'), may hold values from -6 to 6
- gates: float32 [4096, 2], P('expert'), may hold values from 0.2 to 1
- expert_ids: int32 [4096, 2], P('expert'), may hold values from 0 to 15, all different within a row; in each aligned block of 512 rows (0 to 511, 512 to 1023, ...) at most 128 rows name the same one
- up_weight: bfloat16 [16, 768, 3072], P('expert', None, 'ffn'), may hold values from -0.21875 to 0.21875
- down_weight: bfloat16 [16, 3072, 768], P('expert', 'ffn'), may hold values from -0.109375 to 0.109375
Outputs:
- layer_out: bfloat16 [4096, 768], P('expert', 'ffn')
- grad_tokens: bfloat16 [4096, 768], P('expert', 'ffn')
- grad_up: bfloat16 [16, 768, 3072], P('expert', None, 'ffn')
- grad_down: bfloat16 [16, 3072, 768], P('expert', 'ffn')
The draws below stay inside these ranges and needn't reach their ends.
Inputs may be any that keep to these rules, and one draw needn't show every extreme that they name: `expert_ids`: the two experts of a token differ. Among the tokens of one index of expert no expert is named more than 128 times, a bound that some block reaches.
All inputs are finite; a program needn't handle non-finite values.
Results may differ from the reference program's by a relative error of at most 0.0065.
Values may be sent and summed in bfloat16 or wider, within the bound.
A program may use at most 192 MiB of HBM per device.

```python
import math
import jax
import jax.numpy as jnp
import numpy as np
from jax import lax

D = 768
FF = 3072
TOK_DEV = 512
EXPERTS = 16
TOKENS = 4096
CAP = 128
SLOTS = 1024
N_EXPERT = 8


def levels(rng, extent, pieces, least, top_value):
    def one(dim, blocks):
        heights = jax.random.uniform(jax.random.fold_in(jax.random.fold_in(rng, 6), dim), (blocks,), jnp.float32, least / len(pieces), top_value / len(pieces))
        return jnp.repeat(jnp.exp(heights), extent[dim] // blocks).reshape((-1,) + (1,) * (len(extent) - dim - 1))

    factor_of = one(*pieces[0])
    for cut in pieces[1:]:
        factor_of = factor_of * one(*cut)
    return factor_of


def shared_out(key, own, number, rows, number_of, top, reach, skew):
    sequence = jax.random.permutation(key, number_of)
    packed, usual = shares(number_of, rows * top, reach, skew, True), shares(number_of, rows * top, reach, skew, False)
    places = jnp.arange(number_of)

    def named(lengths, turn):
        used = int((lengths > 0).sum())
        fixed = max(1, used // 4)
        shifted = fixed + (places - fixed + turn * (used - fixed)) % max(1, number_of - fixed)
        return jnp.zeros((number_of,), jnp.int32).at[sequence[jnp.where(places < fixed, places, shifted)]].set(jnp.asarray(lengths, jnp.int32))

    lengths = jnp.where(number % 4 == 0, named(packed, number // 4), named(usual, number - number // 4 - 1))
    mixed = jax.random.permutation(jax.random.fold_in(own, 3), number_of)
    source_of, taker = mixed[0:number_of // 2 * 2:2], mixed[1:number_of // 2 * 2:2]
    slack = jnp.minimum(lengths[source_of] - 1, reach - lengths[taker]) // 2
    slack = jnp.where((source_of == sequence[0]) | (taker == sequence[0]) | (lengths[taker] == 0), 0, jnp.maximum(slack, 0))
    shifted = jax.random.randint(jax.random.fold_in(own, 4), (number_of // 2,), 0, 1 << 20) % (slack + 1)
    lengths = lengths.at[source_of].add(-shifted).at[taker].add(shifted)
    items = jnp.searchsorted(jnp.cumsum(lengths), jnp.arange(rows * top), side="right").astype(jnp.int32)
    table = items.reshape(top, rows).T
    table = table[jax.random.permutation(jax.random.fold_in(own, 1), rows)]
    turn = jax.random.randint(jax.random.fold_in(own, 2), (rows, 1), 0, top)
    return jnp.take_along_axis(table, (jnp.arange(top)[None, :] + turn) % top, axis=1)


def shares(number_of, total, bound, slope, full):
    portions = [(1 << 20) // math.isqrt(grade ** slope) + 1 for grade in range(1, number_of + 1)]
    largest = bound if full else min(bound, max(-(-total // number_of), total * portions[0] // sum(portions)))
    least = 1 if total - largest >= number_of - 1 else 0
    counts, surplus = [largest] + [least] * (number_of - 1), total - largest - least * (number_of - 1)
    while surplus > 0:
        movable = [i for i in range(1, number_of) if counts[i] < largest] or [i for i in range(1, number_of) if counts[i] < bound]
        whole, left = sum([portions[i] for i in movable]), surplus
        for i in movable:
            more = min(bound - counts[i], max(1, left * portions[i] // whole), surplus)
            counts[i] = counts[i] + more
            surplus = surplus - more
    return np.array(counts)


def normal_values(own_key, dims, width, reach, pieces=(), kind=jnp.bfloat16):
    values = width * jax.random.normal(own_key, dims, jnp.float32)
    if pieces:
        values = values * levels(own_key, dims, pieces, -0.22, 0.18)
    return jnp.clip(values, -reach, reach).astype(kind)


def setup_inputs(seed: int = 0) -> dict:
    keys = jax.random.split(jax.random.key(seed), 7)
    tokens = normal_values(keys[0], (TOKENS, D), 1.0, 6.0, ((0, 8), (1, 4)))
    cotangent = normal_values(keys[1], (TOKENS, D), 1.0, 6.0, ((0, 8), (1, 4)))
    gates = jnp.clip(jnp.exp(math.log(1.0) - 1.609438 * jax.random.uniform(keys[2], (TOKENS, 2), jnp.float32) ** levels(keys[2], (TOKENS, 2), ((0, 8),), -0.2, 0.2)), 0.2, 1.0)
    expert_ids_keys = jax.random.split(jax.random.fold_in(keys[3], 1), TOKENS // TOK_DEV)
    expert_ids_turns = jax.random.permutation(jax.random.fold_in(keys[3], 3), TOKENS // TOK_DEV)
    expert_ids = jax.vmap(lambda own, number: shared_out(jax.random.fold_in(keys[3], 2), own, number, TOK_DEV, EXPERTS, 2, CAP, 2))(expert_ids_keys, expert_ids_turns).reshape((TOKENS, 2))
    up_weight = normal_values(keys[4], (EXPERTS, D, FF), D ** -0.5, 0.21875, ((0, 8), (2, 4)))
    down_weight = normal_values(keys[5], (EXPERTS, FF, D), FF ** -0.5, 0.109375, ((0, 8), (1, 4)))
    return dict(tokens=tokens, cotangent=cotangent, gates=gates, expert_ids=expert_ids, up_weight=up_weight, down_weight=down_weight)


def reference(tokens, cotangent, gates, expert_ids, up_weight, down_weight):
    per_block = 2 * TOK_DEV
    flat_ids = expert_ids.reshape(N_EXPERT, per_block)
    labels = jnp.arange(EXPERTS, dtype=jnp.int32)
    onehot = (flat_ids[:, :, None] == labels[None, None, :]).astype(jnp.int32)
    before = jnp.cumsum(onehot, axis=1) - onehot
    position = jnp.sum(onehot * before, axis=2)
    slot_row = jnp.arange(N_EXPERT, dtype=jnp.int32)[:, None] * CAP + position
    table_key = (flat_ids * SLOTS + slot_row).reshape(-1)
    lookup = jnp.full((EXPERTS * SLOTS,), -1, jnp.int32).at[table_key].set(jnp.arange(2 * TOKENS, dtype=jnp.int32))
    scaled = (gates.reshape(-1)[:, None] * jnp.repeat(cotangent, 2, axis=0).astype(jnp.float32)).astype(tokens.dtype)
    zero_value = jnp.zeros((), tokens.dtype)

    def one_expert(expert):
        slot_index = lax.dynamic_slice_in_dim(lookup, expert * SLOTS, SLOTS)
        is_live = slot_index >= 0
        safe_index = jnp.where(is_live, slot_index, 0).astype(jnp.int32)
        rows_in = jnp.where(is_live[:, None], tokens[safe_index // 2], zero_value)
        grads_in = jnp.where(is_live[:, None], scaled[safe_index], zero_value)
        up_matrix = up_weight[expert]
        down_matrix = down_weight[expert]
        preact = jnp.dot(rows_in, up_matrix, preferred_element_type=jnp.float32)
        gating = jax.nn.sigmoid(preact)
        activated = (preact * gating).astype(tokens.dtype)
        expert_out = jnp.dot(activated, down_matrix, preferred_element_type=jnp.float32).astype(tokens.dtype)
        back_grad = jnp.dot(grads_in, down_matrix.T, preferred_element_type=jnp.float32)
        pre_grad = (back_grad * gating * (1.0 + preact * (1.0 - gating))).astype(tokens.dtype)
        grad_down = jnp.dot(activated.T, grads_in, preferred_element_type=jnp.float32).astype(tokens.dtype)
        grad_up = jnp.dot(rows_in.T, pre_grad, preferred_element_type=jnp.float32).astype(tokens.dtype)
        expert_in = jnp.dot(pre_grad, up_matrix.T, preferred_element_type=jnp.float32).astype(tokens.dtype)
        return grad_up, grad_down, expert_out, expert_in

    grad_up, grad_down, out_all, in_all = lax.map(one_expert, labels)
    all_ids = expert_ids.reshape(-1)
    all_rows = slot_row.reshape(-1)
    out_pick = out_all[all_ids, all_rows].astype(jnp.float32).reshape(TOKENS, 2, D)
    in_pick = in_all[all_ids, all_rows].astype(jnp.float32).reshape(TOKENS, 2, D)
    layer_out = jnp.sum(gates[:, :, None] * out_pick, axis=1).astype(tokens.dtype)
    grad_tokens = jnp.sum(in_pick, axis=1).astype(tokens.dtype)
    return layer_out, grad_tokens, grad_up, grad_down
```

```python
import jax
import jax.numpy as jnp
from jax import lax
from jax.sharding import PartitionSpec as P

F32, BF16 = jnp.float32, jnp.bfloat16
FFN = 4


def swap(x, bit):
    return lax.ppermute(x, "ffn", [(i, i ^ bit) for i in range(FFN)])


def in_order(index, mine, other, axis):
    return jnp.where(
        index == 0,
        jnp.concatenate([mine, other], axis=axis),
        jnp.concatenate([other, mine], axis=axis),
    )


def half(index, x, axis):
    size = x.shape[axis] // 2
    return lax.dynamic_slice_in_dim(x, index * size, size, axis)


def placers(expert_ids, gates, core, owners, experts, capacity):
    tok = expert_ids.shape[0]
    ids = expert_ids.T
    weight = gates.T
    named = (ids[:, None, :] == lax.broadcasted_iota(jnp.int32, (2, experts, tok), 1)).astype(BF16)
    earlier = (
        lax.broadcasted_iota(jnp.int32, (tok, tok), 0)
        < lax.broadcasted_iota(jnp.int32, (tok, tok), 1)
    ).astype(BF16)
    before = jnp.dot(named[0] + named[1], earlier, preferred_element_type=F32)
    position = jnp.sum(named.astype(F32) * before[None], axis=1).astype(jnp.int32)
    target = jnp.where(ids % 2 == core, (ids // 2) * capacity + position, -1)
    rows = lax.broadcasted_iota(jnp.int32, (owners * capacity, tok), 0)
    first, second = rows == target[0][None], rows == target[1][None]
    gated = jnp.where(first, weight[0][None], 0.0) + jnp.where(second, weight[1][None], 0.0)
    return jnp.logical_or(first, second).astype(BF16), gated


def over_owners(x):
    return lax.all_to_all(x, "expert", split_axis=0, concat_axis=0, tiled=True)


def shards(tokens, cotangent, gates, expert_ids, up_weight, down_weight):
    owners = lax.axis_size("expert")
    local_experts = up_weight.shape[0]
    tok, width = tokens.shape
    capacity = 2 * tok // owners
    ffn = lax.axis_index("ffn")
    core, far = ffn % 2, ffn // 2

    placer, gated = placers(
        expert_ids, gates, core, owners, owners * local_experts, capacity
    )
    both = jnp.concatenate([tokens, cotangent], axis=1)
    mate = swap(both, 1)
    chip_tokens = in_order(core, both[:, :width], mate[:, :width], 1)
    chip_cot = in_order(core, both[:, width:], mate[:, width:], 1)
    sent_rows = jnp.dot(placer, chip_tokens, preferred_element_type=F32).astype(BF16)
    slot_gate = jnp.sum(gated, axis=1, keepdims=True)
    sent_grads = (
        slot_gate * jnp.dot(placer, chip_cot, preferred_element_type=F32)
    ).astype(BF16)

    def dispatched(sent):
        part = over_owners(sent)
        one = in_order(far, part, swap(part, 2), 1)
        return in_order(core, one[None], swap(one, 1)[None], 0)

    rows_in = dispatched(sent_rows)
    grads_in = dispatched(sent_grads)

    def returned(partial):
        one = half(core, partial, 0)[0] + swap(half(1 - core, partial, 0)[0].astype(BF16), 1)
        done = half(far, one, 1) + swap(half(1 - far, one, 1).astype(BF16), 2)
        return over_owners(done.astype(BF16))

    def home(weights, slots):
        return lax.dot_general(
            weights, slots, (((0,), (0,)), ((), ())), preferred_element_type=F32
        )

    def joined(part):
        return (half(core, part, 1) + swap(half(1 - core, part, 1), 1)).astype(BF16)

    preact = jnp.einsum("xrd,xdf->xrf", rows_in, up_weight, preferred_element_type=F32)
    gating = jax.nn.sigmoid(preact)
    activated = (preact * gating).astype(BF16)
    out_part = jnp.einsum("xrf,xfd->xrd", activated, down_weight, preferred_element_type=F32)
    out_home = returned(out_part)
    back_grad = jnp.einsum("xrd,xfd->xrf", grads_in, down_weight, preferred_element_type=F32)
    pre_grad = (back_grad * gating * (1.0 + preact * (1.0 - gating))).astype(BF16)
    in_part = jnp.einsum("xrf,xdf->xrd", pre_grad, up_weight, preferred_element_type=F32)
    in_home = returned(in_part)
    grad_down = jnp.einsum(
        "xrf,xrd->xfd", activated, grads_in, preferred_element_type=F32
    ).astype(BF16)
    grad_up = jnp.einsum("xrd,xrf->xdf", rows_in, pre_grad, preferred_element_type=F32).astype(BF16)

    high = lax.reduce_precision(gated, 8, 7)
    layer_out = joined(
        home(high.astype(BF16), out_home) + home((gated - high).astype(BF16), out_home)
    )
    grad_tokens = joined(home(placer, in_home))
    return (layer_out, grad_tokens, grad_up, grad_down)


def solution(mesh):
    placed = (
        P("expert", "ffn"),
        P("expert", "ffn"),
        P("expert", None),
        P("expert", None),
        P("expert", None, "ffn"),
        P("expert", "ffn", None),
    )
    return jax.shard_map(
        shards,
        mesh=mesh,
        in_specs=placed,
        out_specs=(
            P("expert", "ffn"),
            P("expert", "ffn"),
            P("expert", None, "ffn"),
            P("expert", "ffn", None),
        ),
        check_vma=False,
    )
```

```python
import functools

import jax
import jax.numpy as jnp
from jax import lax
from jax.experimental import pallas as pl
from jax.experimental.pallas import tpu as pltpu
from jax.sharding import PartitionSpec as P

F32, BF16 = jnp.float32, jnp.bfloat16
FFN = 4


def swap(x, bit):
    return lax.ppermute(x, "ffn", [(i, i ^ bit) for i in range(FFN)])


def in_order(index, mine, other, axis):
    return jnp.where(
        index == 0,
        jnp.concatenate([mine, other], axis=axis),
        jnp.concatenate([other, mine], axis=axis),
    )


def half(index, x, axis):
    size = x.shape[axis] // 2
    return lax.dynamic_slice_in_dim(x, index * size, size, axis)


def placers(expert_ids, gates, core, owners, experts, capacity):
    tok = expert_ids.shape[0]
    ids = expert_ids.T
    weight = gates.T
    named = (ids[:, None, :] == lax.broadcasted_iota(jnp.int32, (2, experts, tok), 1)).astype(BF16)
    earlier = (
        lax.broadcasted_iota(jnp.int32, (tok, tok), 0)
        < lax.broadcasted_iota(jnp.int32, (tok, tok), 1)
    ).astype(BF16)
    before = jnp.dot(named[0] + named[1], earlier, preferred_element_type=F32)
    position = jnp.sum(named.astype(F32) * before[None], axis=1).astype(jnp.int32)
    target = jnp.where(ids % 2 == core, (ids // 2) * capacity + position, -1)
    rows = lax.broadcasted_iota(jnp.int32, (owners * capacity, tok), 0)
    first, second = rows == target[0][None], rows == target[1][None]
    gated = jnp.where(first, weight[0][None], 0.0) + jnp.where(second, weight[1][None], 0.0)
    return jnp.logical_or(first, second).astype(BF16), gated


LAG = 2
MESH = pl.DeviceIdType.MESH


def greet(owners, e, f):
    barrier = pltpu.get_barrier_semaphore()

    def tell(s, carry):
        pl.semaphore_signal(
            barrier, inc=1, device_id=(lax.rem(e + s, owners), f), device_id_type=MESH
        )
        return carry

    lax.fori_loop(1, owners, tell, 0)
    for peer in (mate_of(f), far_of(f)):
        pl.semaphore_signal(barrier, inc=1, device_id=(e, peer), device_id_type=MESH)
    pl.semaphore_wait(barrier, owners + 1)


def mate_of(f):
    return f + 1 - 2 * lax.rem(f, 2)


def far_of(f):
    return lax.rem(f + 2, FFN)


def staged(count, first, second):
    def lead(n, carry):
        first(n)
        return carry

    def steady(n, carry):
        first(n)
        second(n - LAG)
        return carry

    def tail(n, carry):
        second(n)
        return carry

    lax.fori_loop(0, LAG, lead, 0)
    lax.fori_loop(LAG, count, steady, 0)
    lax.fori_loop(count - LAG, count, tail, 0)


def each(start, stop, body):
    def step(n, carry):
        body(n)
        return carry

    lax.fori_loop(start, stop, step, 0)


def dispatch_kernel(owners, sent, rows, own_sem, a_send, a_recv, x_send, x_recv, c_send, c_recv):
    e, f = lax.axis_index("expert"), lax.axis_index("ffn")
    core, far = lax.rem(f, 2), f // 2
    cap = sent.shape[1] // owners
    wide = sent.shape[2]
    near = pl.ds(pl.multiple_of(far * wide, wide), wide)

    def block(b):
        return pl.ds(pl.multiple_of(b * cap, cap), cap)

    def across(n):
        t, s = n // owners, lax.rem(n, owners)
        to = lax.rem(e + s, owners)
        return pltpu.make_async_remote_copy(
            src_ref=sent.at[t, block(to)],
            dst_ref=rows.at[t, core, block(e), near],
            send_sem=a_send.at[n],
            recv_sem=a_recv.at[n],
            device_id=(to, f),
            device_id_type=MESH,
        )

    def within(n, peer, columns, send, recv):
        t, s = n // owners, lax.rem(n, owners)
        part = rows.at[t, core, block(lax.rem(e + owners - s, owners)), columns]
        return pltpu.make_async_remote_copy(
            src_ref=part,
            dst_ref=part,
            send_sem=send.at[n],
            recv_sem=recv.at[n],
            device_id=(e, peer),
            device_id_type=MESH,
        )

    def to_far(n):
        return within(n, far_of(f), near, x_send, x_recv)

    def to_mate(n):
        return within(n, mate_of(f), slice(None), c_send, c_recv)

    def own(t):
        return pltpu.make_async_copy(
            sent.at[t, block(e)], rows.at[t, core, block(e), near], own_sem.at[t]
        )

    greet(owners, e, f)
    for t in range(2):
        own(t).start()
        each(t * owners + 1, (t + 1) * owners, lambda n: across(n).start())
    for t in range(2):
        own(t).wait()

    def first(n):
        @pl.when(lax.rem(n, owners) != 0)
        def _():
            across(n).wait_recv()

        to_far(n).start()

    def second(n):
        to_far(n).wait_recv()
        to_mate(n).start()

    staged(2 * owners, first, second)

    def finish(n):
        to_mate(n).wait_recv()
        to_mate(n).wait_send()
        to_far(n).wait_send()

        @pl.when(lax.rem(n, owners) != 0)
        def _():
            across(n).wait_send()

    each(0, 2 * owners, finish)


def dispatch(sent, owners):
    _, count, wide = sent.shape
    return pl.pallas_call(
        functools.partial(dispatch_kernel, owners),
        out_shape=jax.ShapeDtypeStruct((2, 2, count, 2 * wide), BF16),
        in_specs=[pl.BlockSpec(memory_space=pltpu.VMEM)],
        out_specs=pl.BlockSpec(memory_space=pltpu.VMEM),
        scratch_shapes=[pltpu.SemaphoreType.DMA((2,))]
        + [pltpu.SemaphoreType.DMA((2 * owners,))] * 6,
        compiler_params=pltpu.CompilerParams(
            collective_id=0, has_side_effects=True, vmem_limit_bytes=48 * 2**20
        ),
        name="dispatch",
    )(sent)


def return_kernel(
    owners, mine, given, home, from_mate, to_x, from_x, done,
    a_send, a_recv, x_send, x_recv, c_send, c_recv,
):
    e, f = lax.axis_index("expert"), lax.axis_index("ffn")
    far = f // 2
    cap = mine.shape[1] // owners
    wide = mine.shape[2] // 2
    near = pl.ds(pl.multiple_of(far * wide, wide), wide)
    other = pl.ds(pl.multiple_of((1 - far) * wide, wide), wide)

    def block(b):
        return pl.ds(pl.multiple_of(b * cap, cap), cap)

    def place(n):
        return n // owners, block(lax.rem(e + lax.rem(n, owners) + 1, owners))

    def remote(src, dst, send, recv, device):
        return pltpu.make_async_remote_copy(
            src_ref=src, dst_ref=dst, send_sem=send, recv_sem=recv,
            device_id=device, device_id_type=MESH,
        )

    def to_mate(n):
        t, b = place(n)
        return remote(
            given.at[t, b], from_mate.at[t, b], c_send.at[n], c_recv.at[n], (e, mate_of(f))
        )

    def to_far(n):
        t, b = place(n)
        return remote(to_x.at[t, b], from_x.at[t, b], x_send.at[n], x_recv.at[n], (e, far_of(f)))

    def to_home(n):
        t, b = place(n)
        owner = lax.rem(e + lax.rem(n, owners) + 1, owners)
        return remote(
            done.at[t, b], home.at[t, block(e)], a_send.at[n], a_recv.at[n], (owner, f)
        )

    def leaves(n):
        return lax.rem(n, owners) != owners - 1

    greet(owners, e, f)
    each(0, 2 * owners, lambda n: to_mate(n).start())

    def first(n):
        t, b = place(n)
        to_mate(n).wait_recv()
        to_x[t, b, :] = (mine[t, b, other] + from_mate[t, b, other].astype(F32)).astype(BF16)
        to_far(n).start()

    def second(n):
        t, b = place(n)
        to_far(n).wait_recv()
        total = (
            mine[t, b, near] + from_mate[t, b, near].astype(F32) + from_x[t, b, :].astype(F32)
        ).astype(BF16)

        @pl.when(leaves(n))
        def _():
            done[t, b, :] = total
            to_home(n).start()

        @pl.when(jnp.logical_not(leaves(n)))
        def _():
            home[t, b, :] = total

    staged(2 * owners, first, second)

    def finish(n):
        to_mate(n).wait_send()
        to_far(n).wait_send()

        @pl.when(leaves(n))
        def _():
            to_home(n).wait_recv()
            to_home(n).wait_send()

    each(0, 2 * owners, finish)


def give_back(mine, given, owners):
    _, count, width = mine.shape
    narrow = pltpu.VMEM((2, count, width // 2), BF16)
    return pl.pallas_call(
        functools.partial(return_kernel, owners),
        out_shape=jax.ShapeDtypeStruct((2, count, width // 2), BF16),
        in_specs=[pl.BlockSpec(memory_space=pltpu.VMEM)] * 2,
        out_specs=pl.BlockSpec(memory_space=pltpu.VMEM),
        scratch_shapes=[pltpu.VMEM((2, count, width), BF16), narrow, narrow, narrow]
        + [pltpu.SemaphoreType.DMA((2 * owners,))] * 6,
        compiler_params=pltpu.CompilerParams(
            collective_id=1, has_side_effects=True, vmem_limit_bytes=56 * 2**20
        ),
        name="give_back",
    )(mine, given)


def shards(tokens, cotangent, gates, expert_ids, up_weight, down_weight):
    owners = lax.axis_size("expert")
    local_experts = up_weight.shape[0]
    tok, width = tokens.shape
    capacity = 2 * tok // owners
    ffn = lax.axis_index("ffn")
    core, far = ffn % 2, ffn // 2

    placer, gated = placers(
        expert_ids, gates, core, owners, owners * local_experts, capacity
    )
    both = jnp.concatenate([tokens, cotangent], axis=1)
    mate = swap(both, 1)
    chip_tokens = in_order(core, both[:, :width], mate[:, :width], 1)
    chip_cot = in_order(core, both[:, width:], mate[:, width:], 1)
    sent_rows = jnp.dot(placer, chip_tokens, preferred_element_type=F32).astype(BF16)
    slot_gate = jnp.sum(gated, axis=1, keepdims=True)
    sent_grads = (
        slot_gate * jnp.dot(placer, chip_cot, preferred_element_type=F32)
    ).astype(BF16)

    arrived = dispatch(jnp.stack([sent_rows, sent_grads]), owners)
    rows_in, grads_in = arrived[0], arrived[1]

    def home(weights, slots):
        return lax.dot_general(
            weights, slots, (((0,), (0,)), ((), ())), preferred_element_type=F32
        )

    def joined(part):
        return (half(core, part, 1) + swap(half(1 - core, part, 1), 1)).astype(BF16)

    preact = jnp.einsum("xrd,xdf->xrf", rows_in, up_weight, preferred_element_type=F32)
    gating = jax.nn.sigmoid(preact)
    activated = (preact * gating).astype(BF16)
    out_part = jnp.einsum("xrf,xfd->xrd", activated, down_weight, preferred_element_type=F32)
    back_grad = jnp.einsum("xrd,xfd->xrf", grads_in, down_weight, preferred_element_type=F32)
    pre_grad = (back_grad * gating * (1.0 + preact * (1.0 - gating))).astype(BF16)
    in_part = jnp.einsum("xrf,xdf->xrd", pre_grad, up_weight, preferred_element_type=F32)
    parts = jnp.stack([out_part, in_part])
    mine = half(core, parts, 1)[:, 0]
    given = half(1 - core, parts, 1)[:, 0].astype(BF16)
    out_home, in_home = give_back(mine, given, owners)
    grad_down = jnp.einsum(
        "xrf,xrd->xfd", activated, grads_in, preferred_element_type=F32
    ).astype(BF16)
    grad_up = jnp.einsum("xrd,xrf->xdf", rows_in, pre_grad, preferred_element_type=F32).astype(BF16)

    high = lax.reduce_precision(gated, 8, 7)
    layer_out = joined(
        home(high.astype(BF16), out_home) + home((gated - high).astype(BF16), out_home)
    )
    grad_tokens = joined(home(placer, in_home))
    return (layer_out, grad_tokens, grad_up, grad_down)


def solution(mesh):
    placed = (
        P("expert", "ffn"),
        P("expert", "ffn"),
        P("expert", None),
        P("expert", None),
        P("expert", None, "ffn"),
        P("expert", "ffn", None),
    )
    return jax.shard_map(
        shards,
        mesh=mesh,
        in_specs=placed,
        out_specs=(
            P("expert", "ffn"),
            P("expert", "ffn"),
            P("expert", None, "ffn"),
            P("expert", "ffn", None),
        ),
        check_vma=False,
    )
```

```python
import functools

import jax
import jax.numpy as jnp
from jax import lax
from jax.experimental import pallas as pl
from jax.experimental.pallas import tpu as pltpu
from jax.sharding import PartitionSpec as P

F32, BF16 = jnp.float32, jnp.bfloat16
FFN = 4


def swap(x, bit):
    return lax.ppermute(x, "ffn", [(i, i ^ bit) for i in range(FFN)])


def in_order(index, mine, other, axis):
    return jnp.where(
        index == 0,
        jnp.concatenate([mine, other], axis=axis),
        jnp.concatenate([other, mine], axis=axis),
    )


def half(index, x, axis):
    size = x.shape[axis] // 2
    return lax.dynamic_slice_in_dim(x, index * size, size, axis)


def placers(expert_ids, gates, core, owners, experts, capacity):
    tok = expert_ids.shape[0]
    ids = expert_ids.T
    weight = gates.T
    named = (ids[:, None, :] == lax.broadcasted_iota(jnp.int32, (2, experts, tok), 1)).astype(BF16)
    earlier = (
        lax.broadcasted_iota(jnp.int32, (tok, tok), 0)
        < lax.broadcasted_iota(jnp.int32, (tok, tok), 1)
    ).astype(BF16)
    before = jnp.dot(named[0] + named[1], earlier, preferred_element_type=F32)
    position = jnp.sum(named.astype(F32) * before[None], axis=1).astype(jnp.int32)
    target = jnp.where(ids % 2 == core, (ids // 2) * capacity + position, -1)
    rows = lax.broadcasted_iota(jnp.int32, (owners * capacity, tok), 0)
    first, second = rows == target[0][None], rows == target[1][None]
    gated = jnp.where(first, weight[0][None], 0.0) + jnp.where(second, weight[1][None], 0.0)
    return jnp.logical_or(first, second).astype(BF16), gated


LAG = 2
MESH = pl.DeviceIdType.MESH


def greet(owners, e, f):
    barrier = pltpu.get_barrier_semaphore()

    def tell(s, carry):
        pl.semaphore_signal(
            barrier, inc=1, device_id=(lax.rem(e + s, owners), f), device_id_type=MESH
        )
        return carry

    lax.fori_loop(1, owners, tell, 0)
    for peer in (mate_of(f), far_of(f)):
        pl.semaphore_signal(barrier, inc=1, device_id=(e, peer), device_id_type=MESH)
    pl.semaphore_wait(barrier, owners + 1)


def mate_of(f):
    return f + 1 - 2 * lax.rem(f, 2)


def far_of(f):
    return lax.rem(f + 2, FFN)


def staged(count, first, second):
    def lead(n, carry):
        first(n)
        return carry

    def steady(n, carry):
        first(n)
        second(n - LAG)
        return carry

    def tail(n, carry):
        second(n)
        return carry

    lax.fori_loop(0, LAG, lead, 0)
    lax.fori_loop(LAG, count, steady, 0)
    lax.fori_loop(count - LAG, count, tail, 0)


def each(start, stop, body):
    def step(n, carry):
        body(n)
        return carry

    lax.fori_loop(start, stop, step, 0)


def dot(a, b, dims):
    return lax.dot_general(a, b, (dims, ((), ())), preferred_element_type=F32)


def dispatch_kernel(
    owners, sent, up, down, rows, activated, pre_grad, mine, given, preact, own_sem,
    a_send, a_recv, x_send, x_recv, c_send, c_recv,
):
    e, f = lax.axis_index("expert"), lax.axis_index("ffn")
    core, far = lax.rem(f, 2), f // 2
    cap = sent.shape[1] // owners
    wide = sent.shape[2]
    near = pl.ds(pl.multiple_of(far * wide, wide), wide)

    def block(b):
        return pl.ds(pl.multiple_of(b * cap, cap), cap)

    def across(n):
        t, s = n // owners, lax.rem(n, owners)
        to = lax.rem(e + s, owners)
        return pltpu.make_async_remote_copy(
            src_ref=sent.at[t, block(to)],
            dst_ref=rows.at[t, core, block(e), near],
            send_sem=a_send.at[n],
            recv_sem=a_recv.at[n],
            device_id=(to, f),
            device_id_type=MESH,
        )

    def within(n, peer, columns, send, recv):
        t, s = n // owners, lax.rem(n, owners)
        part = rows.at[t, core, block(lax.rem(e + owners - s, owners)), columns]
        return pltpu.make_async_remote_copy(
            src_ref=part,
            dst_ref=part,
            send_sem=send.at[n],
            recv_sem=recv.at[n],
            device_id=(e, peer),
            device_id_type=MESH,
        )

    def to_far(n):
        return within(n, far_of(f), near, x_send, x_recv)

    def to_mate(n):
        return within(n, mate_of(f), slice(None), c_send, c_recv)

    def own(t):
        return pltpu.make_async_copy(
            sent.at[t, block(e)], rows.at[t, core, block(e), near], own_sem.at[t]
        )

    greet(owners, e, f)
    for t in range(2):
        own(t).start()
        each(t * owners + 1, (t + 1) * owners, lambda n: across(n).start())
    for t in range(2):
        own(t).wait()

    def first(n):
        @pl.when(lax.rem(n, owners) != 0)
        def _():
            across(n).wait_recv()

        to_far(n).start()

    def second(n):
        to_far(n).wait_recv()
        to_mate(n).start()

    def forward(m):
        b = block(lax.rem(e + owners - m, owners))
        for x, here in ((core, True), (1 - core, False)):
            pre = dot(rows[0, x, b, :], up[x], ((1,), (0,)))
            preact[x, b, :] = pre
            act = (pre * jax.nn.sigmoid(pre)).astype(BF16)
            activated[x, b, :] = act
            out = dot(act, down[x], ((1,), (0,)))
            if here:
                mine[0, b, :] = out
            else:
                given[0, b, :] = out.astype(BF16)

    def backward(m):
        b = block(lax.rem(e + owners - m, owners))
        for x, here in ((core, True), (1 - core, False)):
            back = dot(rows[1, x, b, :], down[x], ((1,), (1,)))
            pre = preact[x, b, :]
            gating = jax.nn.sigmoid(pre)
            grad = (back * gating * (1.0 + pre * (1.0 - gating))).astype(BF16)
            pre_grad[x, b, :] = grad
            out = dot(grad, up[x], ((1,), (1,)))
            if here:
                mine[1, b, :] = out
            else:
                given[1, b, :] = out.astype(BF16)

    def step(n):
        @pl.when(n < 2 * owners)
        def _():
            first(n)

        @pl.when(jnp.logical_and(n >= LAG, n < 2 * owners + LAG))
        def _():
            second(n - LAG)

        @pl.when(n >= 2 * LAG)
        def _():
            to_mate(n - 2 * LAG).wait_recv()

        @pl.when(jnp.logical_and(n >= 2 * LAG, n < owners + 2 * LAG))
        def _():
            forward(n - 2 * LAG)

        @pl.when(n >= owners + 2 * LAG)
        def _():
            backward(n - owners - 2 * LAG)

    each(0, 2 * owners + 2 * LAG, step)

    def finish(n):
        to_mate(n).wait_send()
        to_far(n).wait_send()

        @pl.when(lax.rem(n, owners) != 0)
        def _():
            across(n).wait_send()

    each(0, 2 * owners, finish)


def dispatch(sent, up, down, owners):
    _, count, wide = sent.shape
    hidden = up.shape[2]
    return pl.pallas_call(
        functools.partial(dispatch_kernel, owners),
        out_shape=[
            jax.ShapeDtypeStruct((2, 2, count, 2 * wide), BF16),
            jax.ShapeDtypeStruct((2, count, hidden), BF16),
            jax.ShapeDtypeStruct((2, count, hidden), BF16),
            jax.ShapeDtypeStruct((2, count, 2 * wide), F32),
            jax.ShapeDtypeStruct((2, count, 2 * wide), BF16),
        ],
        in_specs=[pl.BlockSpec(memory_space=pltpu.VMEM)] * 3,
        out_specs=[pl.BlockSpec(memory_space=pltpu.VMEM)] * 5,
        scratch_shapes=[pltpu.VMEM((2, count, hidden), F32), pltpu.SemaphoreType.DMA((2,))]
        + [pltpu.SemaphoreType.DMA((2 * owners,))] * 6,
        compiler_params=pltpu.CompilerParams(
            collective_id=0, has_side_effects=True, vmem_limit_bytes=56 * 2**20
        ),
        name="dispatch",
    )(sent, up, down)


def return_kernel(
    owners, mine, given, home, from_mate, to_x, from_x, done,
    a_send, a_recv, x_send, x_recv, c_send, c_recv,
):
    e, f = lax.axis_index("expert"), lax.axis_index("ffn")
    far = f // 2
    cap = mine.shape[1] // owners
    wide = mine.shape[2] // 2
    near = pl.ds(pl.multiple_of(far * wide, wide), wide)
    other = pl.ds(pl.multiple_of((1 - far) * wide, wide), wide)

    def block(b):
        return pl.ds(pl.multiple_of(b * cap, cap), cap)

    def place(n):
        return n // owners, block(lax.rem(e + lax.rem(n, owners) + 1, owners))

    def remote(src, dst, send, recv, device):
        return pltpu.make_async_remote_copy(
            src_ref=src, dst_ref=dst, send_sem=send, recv_sem=recv,
            device_id=device, device_id_type=MESH,
        )

    def to_mate(n):
        t, b = place(n)
        return remote(
            given.at[t, b], from_mate.at[t, b], c_send.at[n], c_recv.at[n], (e, mate_of(f))
        )

    def to_far(n):
        t, b = place(n)
        return remote(to_x.at[t, b], from_x.at[t, b], x_send.at[n], x_recv.at[n], (e, far_of(f)))

    def to_home(n):
        t, b = place(n)
        owner = lax.rem(e + lax.rem(n, owners) + 1, owners)
        return remote(
            done.at[t, b], home.at[t, block(e)], a_send.at[n], a_recv.at[n], (owner, f)
        )

    def leaves(n):
        return lax.rem(n, owners) != owners - 1

    greet(owners, e, f)
    each(0, 2 * owners, lambda n: to_mate(n).start())

    def first(n):
        t, b = place(n)
        to_mate(n).wait_recv()
        to_x[t, b, :] = (mine[t, b, other] + from_mate[t, b, other].astype(F32)).astype(BF16)
        to_far(n).start()

    def second(n):
        t, b = place(n)
        to_far(n).wait_recv()
        total = (
            mine[t, b, near] + from_mate[t, b, near].astype(F32) + from_x[t, b, :].astype(F32)
        ).astype(BF16)

        @pl.when(leaves(n))
        def _():
            done[t, b, :] = total
            to_home(n).start()

        @pl.when(jnp.logical_not(leaves(n)))
        def _():
            home[t, b, :] = total

    staged(2 * owners, first, second)

    def finish(n):
        to_mate(n).wait_send()
        to_far(n).wait_send()

        @pl.when(leaves(n))
        def _():
            to_home(n).wait_recv()
            to_home(n).wait_send()

    each(0, 2 * owners, finish)


def give_back(mine, given, owners):
    _, count, width = mine.shape
    narrow = pltpu.VMEM((2, count, width // 2), BF16)
    return pl.pallas_call(
        functools.partial(return_kernel, owners),
        out_shape=jax.ShapeDtypeStruct((2, count, width // 2), BF16),
        in_specs=[pl.BlockSpec(memory_space=pltpu.VMEM)] * 2,
        out_specs=pl.BlockSpec(memory_space=pltpu.VMEM),
        scratch_shapes=[pltpu.VMEM((2, count, width), BF16), narrow, narrow, narrow]
        + [pltpu.SemaphoreType.DMA((2 * owners,))] * 6,
        compiler_params=pltpu.CompilerParams(
            collective_id=1, has_side_effects=True, vmem_limit_bytes=56 * 2**20
        ),
        name="give_back",
    )(mine, given)


def shards(tokens, cotangent, gates, expert_ids, up_weight, down_weight):
    owners = lax.axis_size("expert")
    local_experts = up_weight.shape[0]
    tok, width = tokens.shape
    capacity = 2 * tok // owners
    ffn = lax.axis_index("ffn")
    core, far = ffn % 2, ffn // 2

    placer, gated = placers(
        expert_ids, gates, core, owners, owners * local_experts, capacity
    )
    both = jnp.concatenate([tokens, cotangent], axis=1)
    mate = swap(both, 1)
    chip_tokens = in_order(core, both[:, :width], mate[:, :width], 1)
    chip_cot = in_order(core, both[:, width:], mate[:, width:], 1)
    sent_rows = jnp.dot(placer, chip_tokens, preferred_element_type=F32).astype(BF16)
    slot_gate = jnp.sum(gated, axis=1, keepdims=True)
    sent_grads = (
        slot_gate * jnp.dot(placer, chip_cot, preferred_element_type=F32)
    ).astype(BF16)

    arrived, activated, pre_grad, mine, given = dispatch(
        jnp.stack([sent_rows, sent_grads]), up_weight, down_weight, owners
    )
    rows_in, grads_in = arrived[0], arrived[1]
    out_home, in_home = give_back(mine, given, owners)

    def home(weights, slots):
        return lax.dot_general(
            weights, slots, (((0,), (0,)), ((), ())), preferred_element_type=F32
        )

    def joined(part):
        return (half(core, part, 1) + swap(half(1 - core, part, 1), 1)).astype(BF16)

    grad_down = jnp.einsum(
        "xrf,xrd->xfd", activated, grads_in, preferred_element_type=F32
    ).astype(BF16)
    grad_up = jnp.einsum("xrd,xrf->xdf", rows_in, pre_grad, preferred_element_type=F32).astype(BF16)

    high = lax.reduce_precision(gated, 8, 7)
    layer_out = joined(
        home(high.astype(BF16), out_home) + home((gated - high).astype(BF16), out_home)
    )
    grad_tokens = joined(home(placer, in_home))
    return (layer_out, grad_tokens, grad_up, grad_down)


def solution(mesh):
    placed = (
        P("expert", "ffn"),
        P("expert", "ffn"),
        P("expert", None),
        P("expert", None),
        P("expert", None, "ffn"),
        P("expert", "ffn", None),
    )
    return jax.shard_map(
        shards,
        mesh=mesh,
        in_specs=placed,
        out_specs=(
            P("expert", "ffn"),
            P("expert", "ffn"),
            P("expert", None, "ffn"),
            P("expert", "ffn", None),
        ),
        check_vma=False,
    )
```

```python
import functools

import jax
import jax.numpy as jnp
from jax import lax
from jax.experimental import pallas as pl
from jax.experimental.pallas import tpu as pltpu
from jax.sharding import PartitionSpec as P

F32, BF16 = jnp.float32, jnp.bfloat16
FFN = 4


def swap(x, bit):
    return lax.ppermute(x, "ffn", [(i, i ^ bit) for i in range(FFN)])


def in_order(index, mine, other, axis):
    return jnp.where(
        index == 0,
        jnp.concatenate([mine, other], axis=axis),
        jnp.concatenate([other, mine], axis=axis),
    )


def half(index, x, axis):
    size = x.shape[axis] // 2
    return lax.dynamic_slice_in_dim(x, index * size, size, axis)


def placers(expert_ids, gates, core, owners, experts, capacity):
    tok = expert_ids.shape[0]
    ids = expert_ids.T
    weight = gates.T
    named = (ids[:, None, :] == lax.broadcasted_iota(jnp.int32, (2, experts, tok), 1)).astype(BF16)
    earlier = (
        lax.broadcasted_iota(jnp.int32, (tok, tok), 0)
        < lax.broadcasted_iota(jnp.int32, (tok, tok), 1)
    ).astype(BF16)
    before = jnp.dot(named[0] + named[1], earlier, preferred_element_type=F32)
    position = jnp.sum(named.astype(F32) * before[None], axis=1).astype(jnp.int32)
    target = jnp.where(ids % 2 == core, (ids // 2) * capacity + position, -1)
    rows = lax.broadcasted_iota(jnp.int32, (owners * capacity, tok), 0)
    first, second = rows == target[0][None], rows == target[1][None]
    gated = jnp.where(first, weight[0][None], 0.0) + jnp.where(second, weight[1][None], 0.0)
    return jnp.logical_or(first, second).astype(BF16), gated


LAG = 2
MESH = pl.DeviceIdType.MESH


def greet(owners, e, f):
    barrier = pltpu.get_barrier_semaphore()

    def tell(s, carry):
        pl.semaphore_signal(
            barrier, inc=1, device_id=(lax.rem(e + s, owners), f), device_id_type=MESH
        )
        return carry

    lax.fori_loop(1, owners, tell, 0)
    for peer in (mate_of(f), far_of(f)):
        pl.semaphore_signal(barrier, inc=1, device_id=(e, peer), device_id_type=MESH)
    pl.semaphore_wait(barrier, owners + 1)


def mate_of(f):
    return f + 1 - 2 * lax.rem(f, 2)


def far_of(f):
    return lax.rem(f + 2, FFN)


def staged(count, first, second):
    def lead(n, carry):
        first(n)
        return carry

    def steady(n, carry):
        first(n)
        second(n - LAG)
        return carry

    def tail(n, carry):
        second(n)
        return carry

    lax.fori_loop(0, LAG, lead, 0)
    lax.fori_loop(LAG, count, steady, 0)
    lax.fori_loop(count - LAG, count, tail, 0)


def each(start, stop, body):
    def step(n, carry):
        body(n)
        return carry

    lax.fori_loop(start, stop, step, 0)


def dot(a, b, dims):
    return lax.dot_general(a, b, (dims, ((), ())), preferred_element_type=F32)


def dispatch_kernel(
    owners, sent, up, down, rows, activated, pre_grad, mine, given, preact, own_sem,
    a_send, a_recv, x_send, x_recv, c_send, c_recv,
):
    e, f = lax.axis_index("expert"), lax.axis_index("ffn")
    core, far = lax.rem(f, 2), f // 2
    cap = sent.shape[1] // owners
    wide = sent.shape[2]
    near = pl.ds(pl.multiple_of(far * wide, wide), wide)

    def block(b):
        return pl.ds(pl.multiple_of(b * cap, cap), cap)

    def across(n):
        t, s = n // owners, lax.rem(n, owners)
        to = lax.rem(e + s, owners)
        return pltpu.make_async_remote_copy(
            src_ref=sent.at[t, block(to)],
            dst_ref=rows.at[t, core, block(e), near],
            send_sem=a_send.at[n],
            recv_sem=a_recv.at[n],
            device_id=(to, f),
            device_id_type=MESH,
        )

    def within(n, peer, columns, send, recv):
        t, s = n // owners, lax.rem(n, owners)
        part = rows.at[t, core, block(lax.rem(e + owners - s, owners)), columns]
        return pltpu.make_async_remote_copy(
            src_ref=part,
            dst_ref=part,
            send_sem=send.at[n],
            recv_sem=recv.at[n],
            device_id=(e, peer),
            device_id_type=MESH,
        )

    def to_far(n):
        return within(n, far_of(f), near, x_send, x_recv)

    def to_mate(n):
        return within(n, mate_of(f), slice(None), c_send, c_recv)

    def own(t):
        return pltpu.make_async_copy(
            sent.at[t, block(e)], rows.at[t, core, block(e), near], own_sem.at[t]
        )

    greet(owners, e, f)
    for t in range(2):
        own(t).start()
        each(t * owners + 1, (t + 1) * owners, lambda n: across(n).start())
    for t in range(2):
        own(t).wait()

    def first(n):
        @pl.when(lax.rem(n, owners) != 0)
        def _():
            across(n).wait_recv()

        to_far(n).start()

    def second(n):
        to_far(n).wait_recv()
        to_mate(n).start()

    def forward(m):
        b = block(lax.rem(e + owners - m, owners))
        for x, here in ((core, True), (1 - core, False)):
            pre = dot(rows[0, x, b, :], up[x], ((1,), (0,)))
            preact[x, b, :] = pre
            act = (pre * jax.nn.sigmoid(pre)).astype(BF16)
            activated[x, b, :] = act
            out = dot(act, down[x], ((1,), (0,)))
            if here:
                mine[0, b, :] = out
            else:
                given[0, b, :] = out.astype(BF16)

    def backward(m):
        b = block(lax.rem(e + owners - m, owners))
        for x, here in ((core, True), (1 - core, False)):
            back = dot(rows[1, x, b, :], down[x], ((1,), (1,)))
            pre = preact[x, b, :]
            gating = jax.nn.sigmoid(pre)
            grad = (back * gating * (1.0 + pre * (1.0 - gating))).astype(BF16)
            pre_grad[x, b, :] = grad
            out = dot(grad, up[x], ((1,), (1,)))
            if here:
                mine[1, b, :] = out
            else:
                given[1, b, :] = out.astype(BF16)

    def step(n):
        @pl.when(n < 2 * owners)
        def _():
            first(n)

        @pl.when(jnp.logical_and(n >= LAG, n < 2 * owners + LAG))
        def _():
            second(n - LAG)

        @pl.when(n >= 2 * LAG)
        def _():
            to_mate(n - 2 * LAG).wait_recv()

        @pl.when(jnp.logical_and(n >= 2 * LAG, n < owners + 2 * LAG))
        def _():
            forward(n - 2 * LAG)

        @pl.when(n >= owners + 2 * LAG)
        def _():
            backward(n - owners - 2 * LAG)

    each(0, 2 * owners + 2 * LAG, step)

    def finish(n):
        to_mate(n).wait_send()
        to_far(n).wait_send()

        @pl.when(lax.rem(n, owners) != 0)
        def _():
            across(n).wait_send()

    each(0, 2 * owners, finish)


def dispatch(sent, up, down, owners):
    _, count, wide = sent.shape
    hidden = up.shape[2]
    return pl.pallas_call(
        functools.partial(dispatch_kernel, owners),
        out_shape=[
            jax.ShapeDtypeStruct((2, 2, count, 2 * wide), BF16),
            jax.ShapeDtypeStruct((2, count, hidden), BF16),
            jax.ShapeDtypeStruct((2, count, hidden), BF16),
            jax.ShapeDtypeStruct((2, count, 2 * wide), F32),
            jax.ShapeDtypeStruct((2, count, 2 * wide), BF16),
        ],
        in_specs=[pl.BlockSpec(memory_space=pltpu.VMEM)] * 3,
        out_specs=[pl.BlockSpec(memory_space=pltpu.VMEM)] * 5,
        scratch_shapes=[pltpu.VMEM((2, count, hidden), F32), pltpu.SemaphoreType.DMA((2,))]
        + [pltpu.SemaphoreType.DMA((2 * owners,))] * 6,
        compiler_params=pltpu.CompilerParams(
            collective_id=0, has_side_effects=True, vmem_limit_bytes=56 * 2**20
        ),
        name="dispatch",
    )(sent, up, down)


def return_kernel(
    owners, mine, given, rows_hbm, act_hbm, pre_hbm, home, grad_up, grad_down,
    rows, act, pre, load_sem, from_mate, to_x, from_x, done,
    a_send, a_recv, x_send, x_recv, c_send, c_recv,
):
    e, f = lax.axis_index("expert"), lax.axis_index("ffn")
    far = f // 2
    cap = mine.shape[1] // owners
    wide = mine.shape[2] // 2
    near = pl.ds(pl.multiple_of(far * wide, wide), wide)
    other = pl.ds(pl.multiple_of((1 - far) * wide, wide), wide)

    def block(b):
        return pl.ds(pl.multiple_of(b * cap, cap), cap)

    def place(n):
        return n // owners, block(lax.rem(e + lax.rem(n, owners) + 1, owners))

    def remote(src, dst, send, recv, device):
        return pltpu.make_async_remote_copy(
            src_ref=src, dst_ref=dst, send_sem=send, recv_sem=recv,
            device_id=device, device_id_type=MESH,
        )

    def to_mate(n):
        t, b = place(n)
        return remote(
            given.at[t, b], from_mate.at[t, b], c_send.at[n], c_recv.at[n], (e, mate_of(f))
        )

    def to_far(n):
        t, b = place(n)
        return remote(to_x.at[t, b], from_x.at[t, b], x_send.at[n], x_recv.at[n], (e, far_of(f)))

    def to_home(n):
        t, b = place(n)
        owner = lax.rem(e + lax.rem(n, owners) + 1, owners)
        return remote(
            done.at[t, b], home.at[t, block(e)], a_send.at[n], a_recv.at[n], (owner, f)
        )

    def leaves(n):
        return lax.rem(n, owners) != owners - 1

    greet(owners, e, f)
    each(0, 2 * owners, lambda n: to_mate(n).start())
    loads = [
        pltpu.make_async_copy(src, dst, load_sem.at[i])
        for i, (src, dst) in enumerate(((rows_hbm, rows), (act_hbm, act), (pre_hbm, pre)))
    ]
    for load in loads:
        load.start()
    chunks = act.shape[2] // 128

    def first(n):
        t, b = place(n)
        to_mate(n).wait_recv()
        to_x[t, b, :] = (mine[t, b, other] + from_mate[t, b, other].astype(F32)).astype(BF16)
        to_far(n).start()

    def second(n):
        t, b = place(n)
        to_far(n).wait_recv()
        total = (
            mine[t, b, near] + from_mate[t, b, near].astype(F32) + from_x[t, b, :].astype(F32)
        ).astype(BF16)

        @pl.when(leaves(n))
        def _():
            done[t, b, :] = total
            to_home(n).start()

        @pl.when(jnp.logical_not(leaves(n)))
        def _():
            home[t, b, :] = total

    def gradients(q):
        x, part = q // chunks, pl.ds(pl.multiple_of(lax.rem(q, chunks) * 128, 128), 128)
        grad_down[x, part, :] = dot(act[x, :, part], rows[1, x], ((0,), (0,))).astype(BF16)
        grad_up[x, part, :] = dot(rows[0, x, :, part], pre[x], ((0,), (0,))).astype(BF16)

    def both(n):
        second(n)

        @pl.when(n == 0)
        def _():
            for load in loads:
                load.wait()

        @pl.when(n < 2 * chunks)
        def _():
            gradients(n)

    staged(2 * owners, first, both)

    def finish(n):
        to_mate(n).wait_send()
        to_far(n).wait_send()

        @pl.when(leaves(n))
        def _():
            to_home(n).wait_recv()
            to_home(n).wait_send()

    each(0, 2 * owners, finish)


def give_back(mine, given, rows, act, pre, owners):
    _, count, width = mine.shape
    narrow = pltpu.VMEM((2, count, width // 2), BF16)
    return pl.pallas_call(
        functools.partial(return_kernel, owners),
        out_shape=[
            jax.ShapeDtypeStruct((2, count, width // 2), BF16),
            jax.ShapeDtypeStruct((2, width, act.shape[2]), BF16),
            jax.ShapeDtypeStruct((2, act.shape[2], width), BF16),
        ],
        in_specs=[pl.BlockSpec(memory_space=pltpu.VMEM)] * 2
        + [pl.BlockSpec(memory_space=pl.ANY)] * 3,
        out_specs=[pl.BlockSpec(memory_space=pltpu.VMEM)] * 3,
        scratch_shapes=[
            pltpu.VMEM(rows.shape, BF16),
            pltpu.VMEM(act.shape, BF16),
            pltpu.VMEM(pre.shape, BF16),
            pltpu.SemaphoreType.DMA((3,)),
        ]
        + [pltpu.VMEM((2, count, width), BF16), narrow, narrow, narrow]
        + [pltpu.SemaphoreType.DMA((2 * owners,))] * 6,
        compiler_params=pltpu.CompilerParams(
            collective_id=1, has_side_effects=True, vmem_limit_bytes=56 * 2**20
        ),
        name="give_back",
    )(mine, given, rows, act, pre)


def shards(tokens, cotangent, gates, expert_ids, up_weight, down_weight):
    owners = lax.axis_size("expert")
    local_experts = up_weight.shape[0]
    tok, width = tokens.shape
    capacity = 2 * tok // owners
    ffn = lax.axis_index("ffn")
    core, far = ffn % 2, ffn // 2

    placer, gated = placers(
        expert_ids, gates, core, owners, owners * local_experts, capacity
    )
    both = jnp.concatenate([tokens, cotangent], axis=1)
    mate = swap(both, 1)
    chip_tokens = in_order(core, both[:, :width], mate[:, :width], 1)
    chip_cot = in_order(core, both[:, width:], mate[:, width:], 1)
    sent_rows = jnp.dot(placer, chip_tokens, preferred_element_type=F32).astype(BF16)
    slot_gate = jnp.sum(gated, axis=1, keepdims=True)
    sent_grads = (
        slot_gate * jnp.dot(placer, chip_cot, preferred_element_type=F32)
    ).astype(BF16)

    arrived, activated, pre_grad, mine, given = dispatch(
        jnp.stack([sent_rows, sent_grads]), up_weight, down_weight, owners
    )
    homes, grad_up, grad_down = give_back(mine, given, arrived, activated, pre_grad, owners)
    out_home, in_home = homes[0], homes[1]

    def home(weights, slots):
        return lax.dot_general(
            weights, slots, (((0,), (0,)), ((), ())), preferred_element_type=F32
        )

    def joined(part):
        return (half(core, part, 1) + swap(half(1 - core, part, 1), 1)).astype(BF16)

    high = lax.reduce_precision(gated, 8, 7)
    layer_out = joined(
        home(high.astype(BF16), out_home) + home((gated - high).astype(BF16), out_home)
    )
    grad_tokens = joined(home(placer, in_home))
    return (layer_out, grad_tokens, grad_up, grad_down)


def solution(mesh):
    placed = (
        P("expert", "ffn"),
        P("expert", "ffn"),
        P("expert", None),
        P("expert", None),
        P("expert", None, "ffn"),
        P("expert", "ffn", None),
    )
    return jax.shard_map(
        shards,
        mesh=mesh,
        in_specs=placed,
        out_specs=(
            P("expert", "ffn"),
            P("expert", "ffn"),
            P("expert", None, "ffn"),
            P("expert", "ffn", None),
        ),
        check_vma=False,
    )
```
